32 devices in a mesh: groups: 2 (over x), seq: 8 (over z, y), head: 2 (over core).
Axes of the slice: x: 2, y: 2, z: 4, core: 2. Of those that a mesh axis runs over, the one named last changes fastest.
Arguments:
- queries: float32 [4096, 2048], P(('groups', 'seq'), 'head'), parts along dimension 0, may hold values from -6 to 6
- keys: float32 [4096, 2048], P(('groups', 'seq'), 'head'), parts along dimension 0, may hold values from -0.01171875 to 0.01171875
- values: float32 [4096, 2048], P(('groups', 'seq'), 'head'), parts along dimension 0, may hold values from -6 to 6
- level_weight: float32 [16, 6, 4096], P('head', None, ('groups', 'seq')), parts along dimension 2, may hold values from 0.1 to 1
- prefix_weight: float32 [16, 8, 4096], P('head', None, ('groups', 'seq')), parts along dimension 2, may hold values from 0.1 to 1
- prefix_state: float32 [16, 2048, 128], P('head', 'groups'), parts along dimension 1, may hold values from -0.5 to 0.5
Outputs:
- attended: float32 [4096, 2048], P(('groups', 'seq'), 'head'), parts along dimension 0
The draws below stay inside these ranges and needn't reach their ends.
There are 2 independent parts, one for each index of `groups`. The reference program is written for one: setup_inputs(seed, part) draws one part's arguments, and reference() takes and returns one part's arrays. A program takes and returns all parts, laid end to end along the dimension named above; each array names one. Nothing has to cross between parts.
All inputs are finite; a program needn't handle non-finite values.
Results may differ from the reference program's by a relative error of at most 0.00005.
Values sent between devices are 32-bit elements; how exact they have to be, the bound alone decides.
A program may use at most 128 MiB of HBM per device.

```python
import jax
import jax.numpy as jnp
from jax import lax

H = 16
DH = 128
LEVELS = 6
BUCKETS = 8
TOK_DEV = 256
TOKENS = 2048
N_SEQ = 8


def level_of(rng, extent, pieces, least, high):
    loudness, own = 1.0, jax.random.fold_in(rng, 6)
    for position, parts in pieces:
        heights = jnp.exp(jax.random.uniform(jax.random.fold_in(own, position), (parts,), jnp.float32, least / len(pieces), high / len(pieces)))
        loudness = loudness * jnp.repeat(heights, extent[position] // parts).reshape([-1 if axis == position else 1 for axis in range(len(extent))])
    return loudness


def bell_draw(key, shape, spread, limit, cuts=(), kind=jnp.bfloat16):
    level = level_of(key, shape, cuts, -0.22, 0.18) if cuts else 1.0
    values = jax.random.normal(key, shape, jnp.float32) * spread * level
    return jnp.minimum(jnp.maximum(values, -limit), limit).astype(kind)


def setup_inputs(seed: int = 0, part: int = 0) -> dict:
    streams_of = jax.random.split(jax.random.key(seed), 7)
    part_splits = jax.random.split(jax.random.fold_in(streams_of[6], part), 7)
    return {
        "queries": bell_draw(part_splits[0], (TOKENS, H * DH), 1.0, 6.0, ((0, 8), (1, 2)), jnp.float32),
        "keys": bell_draw(part_splits[1], (TOKENS, H * DH), ((DH * TOKENS) ** -0.5), 0.01171875, ((0, 8), (1, 2)), jnp.float32),
        "values": bell_draw(part_splits[2], (TOKENS, H * DH), 1.0, 6.0, ((0, 8), (1, 2)), jnp.float32),
        "level_weight": jnp.clip(0.1 + 0.9 * jax.random.uniform(part_splits[3], (H, LEVELS, TOKENS), jnp.float32) ** level_of(part_splits[3], (H, LEVELS, TOKENS), ((0, 2), (2, 8)), -0.2, 0.2), 0.1, 1.0),
        "prefix_weight": jnp.clip(0.1 + 0.9 * jax.random.uniform(part_splits[4], (H, BUCKETS, TOKENS), jnp.float32) ** level_of(part_splits[4], (H, BUCKETS, TOKENS), ((0, 2), (2, 8)), -0.2, 0.2), 0.1, 1.0),
        "prefix_state": bell_draw(part_splits[5], (H, BUCKETS * DH, DH), DH ** -0.5, 0.5, ((0, 2),), jnp.float32),
    }


def bucket_select():
    block_ids = jnp.arange(N_SEQ, dtype=jnp.int32)
    differing = jnp.bitwise_xor(block_ids[:, None], block_ids[None, :])
    bucket_level_number = sum((jnp.right_shift(differing, shift_by) > 0).astype(jnp.int32) for shift_by in range(LEVELS))
    level_ids = jnp.arange(1, LEVELS, dtype=jnp.int32)
    earlier = (block_ids[None, :] < block_ids[:, None])[:, None, :]
    return earlier & (bucket_level_number[:, None, :] == level_ids[None, :, None])


def one_head(inputs):
    query_heads, key_head_count, value_heads, level_rows, prefix_rows, prefix_mats = inputs
    highest_level = lax.Precision.HIGHEST
    level_selection_mask = bucket_select().astype(query_heads.dtype)
    block_memory_state = jnp.einsum('ctd,cte->cde', key_head_count, value_heads, precision=highest_level)
    per_level_states = jnp.einsum('qov,vfn->qofn', level_selection_mask, block_memory_state, precision=highest_level)
    query_key_scores = jnp.einsum('ctd,csd->cts', query_heads, key_head_count, precision=highest_level)
    row_index = lax.broadcasted_iota(jnp.int32, (TOK_DEV, TOK_DEV), 0)
    col_index = lax.broadcasted_iota(jnp.int32, (TOK_DEV, TOK_DEV), 1)
    causal = col_index <= row_index
    query_key_scores = jnp.where(causal[None], query_key_scores, jnp.zeros_like(query_key_scores)) * level_rows[0][:, :, None]
    local_out = jnp.einsum('cts,cse->cte', query_key_scores, value_heads, precision=highest_level)
    scaled = query_heads[:, None] * jnp.transpose(level_rows[1:], (1, 0, 2))[..., None]
    level_out = jnp.einsum('cltd,clde->cte', scaled, per_level_states, precision=highest_level)
    weighted = query_heads[None] * prefix_rows[..., None]
    prefix_out = jnp.einsum('bctd,bde->cte', weighted, prefix_mats, precision=highest_level)
    return local_out + level_out + prefix_out


def reference(queries, keys, values, level_weight, prefix_weight, prefix_state):
    def split_heads(array):
        return jnp.transpose(array.reshape(N_SEQ, TOK_DEV, H, DH), (2, 0, 1, 3))

    level_rows = level_weight.reshape(H, LEVELS, N_SEQ, TOK_DEV)
    prefix_rows = prefix_weight.reshape(H, BUCKETS, N_SEQ, TOK_DEV)
    prefix_mats = prefix_state.reshape(H, BUCKETS, DH, DH)
    attention_output = lax.map(one_head, (split_heads(queries), split_heads(keys), split_heads(values), level_rows, prefix_rows, prefix_mats))
    return jnp.transpose(attention_output, (1, 2, 0, 3)).reshape(TOKENS, H * DH)
```

```python
import functools

import jax
import jax.numpy as jnp
from jax import lax
from jax.experimental import pallas as pl
from jax.experimental.pallas import tpu as pltpu
from jax.sharding import PartitionSpec as P

DH = 128
WEIGHTS = 16
F32 = jnp.float32
BF16 = jnp.bfloat16


def halves(x):
    high = x.astype(BF16)
    return high, (x - high.astype(F32)).astype(BF16)


def left(x, axis):
    high, low = halves(x)
    return jnp.concatenate([high, low, high], axis=axis)


def right(x, axis):
    high, low = halves(x)
    return jnp.concatenate([high, high, low], axis=axis)


def dot(a, b, dims):
    return lax.dot_general(a, b, (dims, ((), ())), preferred_element_type=F32)


def kernel(
    n, q_hbm, k_hbm, v_hbm, lw_hbm, pw_hbm, ps_hbm, o_hbm,
    q, k, v, lw, pw, ps, acc, wt, run, got, top,
    in_sem, send_sem, recv_sem, top_send, top_recv, out_sem,
):
    bits = n.bit_length() - 1
    stages = bits - 1
    rows = q.shape[0]
    heads = q.shape[1] // DH
    buckets = pw.shape[1]
    me = lax.axis_index("seq")

    def device(position):
        return {"seq": position}

    def cols(h):
        return pl.ds(pl.multiple_of(h * DH, DH), DH)

    def bit(b):
        return jnp.bitwise_and(jnp.right_shift(me, b), 1) == 1

    partners = [jnp.bitwise_xor(me, 1 << b) for b in range(stages)]
    source = (me >= n // 2 - 2) & (me < n // 2)
    upper = me >= n // 2
    onward = (me >= n // 2 - 2) & (me < n - 2)

    loads = [
        pltpu.make_async_copy(a, b, in_sem.at[i])
        for i, (a, b) in enumerate(
            [(k_hbm, k), (v_hbm, v), (q_hbm, q), (lw_hbm, lw), (pw_hbm, pw), (ps_hbm, ps)]
        )
    ]
    for load in loads:
        load.start()

    barrier = pltpu.get_barrier_semaphore()
    for partner in partners:
        pl.semaphore_signal(barrier, inc=1, device_id=device(partner))

    @pl.when(onward)
    def _():
        pl.semaphore_signal(barrier, inc=1, device_id=device(jnp.minimum(me + 2, n - 1)))

    @pl.when(upper)
    def _():
        pl.semaphore_signal(barrier, inc=1, device_id=device(jnp.maximum(me - 2, 0)))

    pl.semaphore_wait(barrier, stages + onward.astype(jnp.int32) + upper.astype(jnp.int32))

    def stage_copy(b, h):
        return pltpu.make_async_remote_copy(
            src_ref=run.at[b, h], dst_ref=got.at[b, h],
            send_sem=send_sem.at[b, h], recv_sem=recv_sem.at[b, h],
            device_id=device(partners[b]),
        )

    def sends(b):
        return jnp.logical_not(bit(b)) if 0 < b == stages - 1 else None

    def receives(b):
        return bit(b) if 0 < b == stages - 1 else None

    def when(cond, fn):
        if cond is None:
            fn()
        else:
            pl.when(cond)(fn)

    def onward_copy(src, h):
        return pltpu.make_async_remote_copy(
            src_ref=src, dst_ref=top.at[h],
            send_sem=top_send.at[0, h], recv_sem=top_recv.at[h],
            device_id=device(jnp.minimum(me + 2, n - 1)),
        )

    def cross_copy(h):
        return pltpu.make_async_remote_copy(
            src_ref=top.at[h], dst_ref=top.at[h],
            send_sem=top_send.at[1, h], recv_sem=top_recv.at[h],
            device_id=device(partners[0]),
        )

    def owner(h):
        return jnp.bitwise_and(h, 1) == jnp.bitwise_and(me, 1)

    loads[0].wait()
    loads[1].wait()

    def states(h, _):
        kh = left(k[:, cols(h)], 0)
        vh = right(v[:, cols(h)], 0)
        run[0, h] = dot(kh, vh, ((0,), (0,)))
        stage_copy(0, h).start()
        return 0

    lax.fori_loop(0, heads, states, 0)

    for load in loads[2:]:
        load.wait()

    def add_level(h, state, index):
        qh = left(q[:, cols(h)], 1)
        acc[:, cols(h)] += wt[h, :, index : index + 1] * dot(qh, right(state, 0), ((1,), (0,)))

    def own(h):
        lv = jnp.concatenate(
            [pw[h], lw[h], jnp.zeros((WEIGHTS - buckets - lw.shape[1], rows), F32)], axis=0
        )
        weights = lv.T
        wt[h, :, 0:WEIGHTS] = weights
        qh = left(q[:, cols(h)], 1)
        kh = right(k[:, cols(h)], 1)
        scores = dot(qh, kh, ((1,), (1,)))
        row = lax.broadcasted_iota(jnp.int32, (rows, rows), 0)
        col = lax.broadcasted_iota(jnp.int32, (rows, rows), 1)
        scores = jnp.where(col <= row, scores, 0.0)
        total = weights[:, buckets : buckets + 1] * dot(
            left(scores, 1), right(v[:, cols(h)], 0), ((1,), (0,))
        )
        for b in range(0, buckets, 2):
            pair = jnp.concatenate(
                [ps[h, c * DH : (c + 1) * DH, :] for c in (b, b + 1)], axis=1
            )
            both = dot(qh, right(pair, 0), ((1,), (0,)))
            total += weights[:, b : b + 1] * both[:, :DH]
            total += weights[:, b + 1 : b + 2] * both[:, DH:]
        acc[:, cols(h)] = total

    def stage(b, h):
        def arrived():
            stage_copy(b, h).wait_recv()
            if b < stages - 1:
                run[b + 1, h] = run[b, h] + got[b, h]
                when(sends(b + 1), lambda: stage_copy(b + 1, h).start())
            else:
                @pl.when(source & owner(h))
                def _():
                    run[b + 1, h] = run[b, h] + got[b, h]
                    onward_copy(run.at[b + 1, h], h).start()

        when(receives(b), arrived)

        @pl.when(bit(b))
        def _():
            add_level(h, got[b, h], buckets + 1 + b)

    def relay(h):
        @pl.when(upper & owner(h))
        def _():
            cross_copy(h).wait_recv()

            @pl.when(onward)
            def _():
                onward_copy(top.at[h], h).start()

            cross_copy(h).start()

    def out_copy(h):
        return pltpu.make_async_copy(acc.at[:, cols(h)], o_hbm.at[:, cols(h)], out_sem.at[h])

    def finish(h):
        @pl.when(upper)
        def _():
            @pl.when(jnp.logical_not(owner(h)))
            def _():
                cross_copy(h).wait_recv()

            add_level(h, top[h], buckets + stages + 1)

        out_copy(h).start()

    def at(h, fn):
        @pl.when((h >= 0) & (h < heads))
        def _():
            fn(h)

    def step(i, _):
        at(i, own)
        for b in range(stages):
            at(i - b, functools.partial(stage, b))
        at(i - stages, relay)
        at(i - stages - 2, finish)
        return 0

    lax.fori_loop(0, heads + stages + 2, step, 0)

    def drain(h, _):
        for b in range(stages):
            when(sends(b), lambda b=b: stage_copy(b, h).wait_send())

        @pl.when(onward & owner(h))
        def _():
            onward_copy(top.at[h], h).wait_send()

        @pl.when(upper & owner(h))
        def _():
            cross_copy(h).wait_send()

        out_copy(h).wait()
        return 0

    lax.fori_loop(0, heads, drain, 0)


def shards(n, queries, keys, values, level_weight, prefix_weight, prefix_state):
    rows, width = queries.shape
    heads = width // DH
    bits = n.bit_length() - 1
    stages = bits - 1
    args = (queries, keys, values, level_weight, prefix_weight, prefix_state)
    state = (heads, DH, DH)
    return pl.pallas_call(
        functools.partial(kernel, n),
        out_shape=jax.ShapeDtypeStruct((rows, width), F32),
        in_specs=[pl.BlockSpec(memory_space=pl.ANY)] * len(args),
        out_specs=pl.BlockSpec(memory_space=pl.ANY),
        scratch_shapes=[pltpu.VMEM(a.shape, F32) for a in args]
        + [
            pltpu.VMEM((rows, width), F32),
            pltpu.VMEM((heads, rows, 128), F32),
            pltpu.VMEM((stages + 1,) + state, F32),
            pltpu.VMEM((stages,) + state, F32),
            pltpu.VMEM(state, F32),
            pltpu.SemaphoreType.DMA((len(args),)),
            pltpu.SemaphoreType.DMA((stages, heads)),
            pltpu.SemaphoreType.DMA((stages, heads)),
            pltpu.SemaphoreType.DMA((2, heads)),
            pltpu.SemaphoreType.DMA((heads,)),
            pltpu.SemaphoreType.DMA((heads,)),
        ],
        compiler_params=pltpu.CompilerParams(
            collective_id=0, has_side_effects=True, vmem_limit_bytes=40 << 20
        ),
        cost_estimate=pl.CostEstimate(flops=2 << 30, bytes_accessed=8 << 20, transcendentals=0),
    )(*args)


def solution(mesh):
    return jax.shard_map(
        functools.partial(shards, mesh.shape["seq"]),
        mesh=mesh,
        in_specs=(
            P(("groups", "seq"), "head"),
            P(("groups", "seq"), "head"),
            P(("groups", "seq"), "head"),
            P("head", None, ("groups", "seq")),
            P("head", None, ("groups", "seq")),
            P("head", "groups", None),
        ),
        out_specs=P(("groups", "seq"), "head"),
        check_vma=False,
    )
```

```python
import functools

import jax
import jax.numpy as jnp
from jax import lax
from jax.experimental import pallas as pl
from jax.experimental.pallas import tpu as pltpu
from jax.sharding import PartitionSpec as P

DH = 128
WEIGHTS = 16
F32 = jnp.float32
BF16 = jnp.bfloat16


def halves(x):
    high = x.astype(BF16)
    return high, (x - high.astype(F32)).astype(BF16)


def left(x, axis):
    high, low = halves(x)
    return jnp.concatenate([high, low, high], axis=axis)


def right(x, axis):
    high, low = halves(x)
    return jnp.concatenate([high, high, low], axis=axis)


def dot(a, b, dims):
    return lax.dot_general(a, b, (dims, ((), ())), preferred_element_type=F32)


def kernel(
    n, q_hbm, k_hbm, v_hbm, lw_hbm, pw_hbm, ps_hbm, o_hbm,
    q, k, v, lw, pw, ps, acc, wt, run, got, top,
    in_sem, send_sem, recv_sem, top_send, top_recv, out_sem,
):
    bits = n.bit_length() - 1
    stages = bits - 1
    rows = q.shape[0]
    heads = q.shape[1] // DH
    buckets = pw.shape[1]
    me = lax.axis_index("seq")

    def device(position):
        return {"seq": position}

    def cols(h):
        return pl.ds(pl.multiple_of(h * DH, DH), DH)

    def bit(b):
        return jnp.bitwise_and(jnp.right_shift(me, b), 1) == 1

    partners = [jnp.bitwise_xor(me, 1 << b) for b in range(stages)]
    source = (me >= n // 2 - 2) & (me < n // 2)
    upper = me >= n // 2
    onward = (me >= n // 2 - 2) & (me < n - 2)

    loads = [
        pltpu.make_async_copy(a, b, in_sem.at[i])
        for i, (a, b) in enumerate(
            [(k_hbm, k), (v_hbm, v), (q_hbm, q), (lw_hbm, lw), (pw_hbm, pw), (ps_hbm, ps)]
        )
    ]
    for load in loads:
        load.start()

    barrier = pltpu.get_barrier_semaphore()
    for partner in partners:
        pl.semaphore_signal(barrier, inc=1, device_id=device(partner))

    @pl.when(onward)
    def _():
        pl.semaphore_signal(barrier, inc=1, device_id=device(jnp.minimum(me + 2, n - 1)))

    @pl.when(upper)
    def _():
        pl.semaphore_signal(barrier, inc=1, device_id=device(jnp.maximum(me - 2, 0)))

    pl.semaphore_wait(barrier, stages + onward.astype(jnp.int32) + upper.astype(jnp.int32))

    def stage_copy(b, h):
        return pltpu.make_async_remote_copy(
            src_ref=run.at[b, h], dst_ref=got.at[b, h],
            send_sem=send_sem.at[b, h], recv_sem=recv_sem.at[b, h],
            device_id=device(partners[b]),
        )

    def sends(b):
        return jnp.logical_not(bit(b)) if 0 < b == stages - 1 else None

    def receives(b):
        return bit(b) if 0 < b == stages - 1 else None

    def when(cond, fn):
        if cond is None:
            fn()
        else:
            pl.when(cond)(fn)

    def onward_copy(src, h):
        return pltpu.make_async_remote_copy(
            src_ref=src, dst_ref=top.at[h],
            send_sem=top_send.at[0, h], recv_sem=top_recv.at[h],
            device_id=device(jnp.minimum(me + 2, n - 1)),
        )

    def cross_copy(h):
        return pltpu.make_async_remote_copy(
            src_ref=top.at[h], dst_ref=top.at[h],
            send_sem=top_send.at[1, h], recv_sem=top_recv.at[h],
            device_id=device(partners[0]),
        )

    def owner(h):
        return jnp.bitwise_and(h, 1) == jnp.bitwise_and(me, 1)

    loads[0].wait()
    loads[1].wait()

    def states(h, _):
        kh = left(k[:, cols(h)], 0)
        vh = right(v[:, cols(h)], 0)
        run[0, h] = dot(kh, vh, ((0,), (0,)))
        stage_copy(0, h).start()
        return 0

    lax.fori_loop(0, heads, states, 0)

    for load in loads[2:]:
        load.wait()

    def add_level(h, state, index):
        qh = left(q[:, cols(h)], 1)
        acc[:, cols(h)] += wt[h, :, index : index + 1] * dot(qh, right(state, 0), ((1,), (0,)))

    def own(h):
        lv = jnp.concatenate(
            [pw[h]]
            + [lw[level, pl.ds(h, 1), :] for level in range(lw.shape[0])]
            + [jnp.zeros((WEIGHTS - buckets - lw.shape[0], rows), F32)],
            axis=0,
        )
        weights = lv.T
        wt[h, :, 0:WEIGHTS] = weights
        qh = left(q[:, cols(h)], 1)
        kh = right(k[:, cols(h)], 1)
        scores = dot(qh, kh, ((1,), (1,)))
        row = lax.broadcasted_iota(jnp.int32, (rows, rows), 0)
        col = lax.broadcasted_iota(jnp.int32, (rows, rows), 1)
        scores = jnp.where(col <= row, scores, 0.0)
        total = weights[:, buckets : buckets + 1] * dot(
            left(scores, 1), right(v[:, cols(h)], 0), ((1,), (0,))
        )
        for b in range(0, buckets, 2):
            pair = jnp.concatenate(
                [ps[h, c * DH : (c + 1) * DH, :] for c in (b, b + 1)], axis=1
            )
            both = dot(qh, right(pair, 0), ((1,), (0,)))
            total += weights[:, b : b + 1] * both[:, :DH]
            total += weights[:, b + 1 : b + 2] * both[:, DH:]
        acc[:, cols(h)] = total

    def stage(b, h):
        def arrived():
            stage_copy(b, h).wait_recv()
            if b < stages - 1:
                run[b + 1, h] = run[b, h] + got[b, h]
                when(sends(b + 1), lambda: stage_copy(b + 1, h).start())
            else:
                @pl.when(source & owner(h))
                def _():
                    run[b + 1, h] = run[b, h] + got[b, h]
                    onward_copy(run.at[b + 1, h], h).start()

        when(receives(b), arrived)

        @pl.when(bit(b))
        def _():
            add_level(h, got[b, h], buckets + 1 + b)

    def relay(h):
        @pl.when(upper & owner(h))
        def _():
            cross_copy(h).wait_recv()

            @pl.when(onward)
            def _():
                onward_copy(top.at[h], h).start()

            cross_copy(h).start()

    def out_copy(h):
        return pltpu.make_async_copy(acc.at[:, cols(h)], o_hbm.at[:, cols(h)], out_sem.at[h])

    def finish(h):
        @pl.when(upper)
        def _():
            @pl.when(jnp.logical_not(owner(h)))
            def _():
                cross_copy(h).wait_recv()

            add_level(h, top[h], buckets + stages + 1)

        out_copy(h).start()

    def at(h, fn):
        @pl.when((h >= 0) & (h < heads))
        def _():
            fn(h)

    def step(i, _):
        at(i, own)
        for b in range(stages):
            at(i - b, functools.partial(stage, b))
        at(i - stages, relay)
        at(i - stages - 2, finish)
        return 0

    lax.fori_loop(0, heads + stages + 2, step, 0)

    def drain(h, _):
        for b in range(stages):
            when(sends(b), lambda b=b: stage_copy(b, h).wait_send())

        @pl.when(onward & owner(h))
        def _():
            onward_copy(top.at[h], h).wait_send()

        @pl.when(upper & owner(h))
        def _():
            cross_copy(h).wait_send()

        out_copy(h).wait()
        return 0

    lax.fori_loop(0, heads, drain, 0)


def shards(n, queries, keys, values, level_weight, prefix_weight, prefix_state):
    rows, width = queries.shape
    heads = width // DH
    bits = n.bit_length() - 1
    stages = bits - 1
    by_level = jnp.transpose(level_weight, (1, 0, 2))
    args = (queries, keys, values, by_level, prefix_weight, prefix_state)
    state = (heads, DH, DH)
    return pl.pallas_call(
        functools.partial(kernel, n),
        out_shape=jax.ShapeDtypeStruct((rows, width), F32),
        in_specs=[pl.BlockSpec(memory_space=pl.ANY)] * len(args),
        out_specs=pl.BlockSpec(memory_space=pl.ANY),
        scratch_shapes=[pltpu.VMEM(a.shape, F32) for a in args]
        + [
            pltpu.VMEM((rows, width), F32),
            pltpu.VMEM((heads, rows, 128), F32),
            pltpu.VMEM((stages + 1,) + state, F32),
            pltpu.VMEM((stages,) + state, F32),
            pltpu.VMEM(state, F32),
            pltpu.SemaphoreType.DMA((len(args),)),
            pltpu.SemaphoreType.DMA((stages, heads)),
            pltpu.SemaphoreType.DMA((stages, heads)),
            pltpu.SemaphoreType.DMA((2, heads)),
            pltpu.SemaphoreType.DMA((heads,)),
            pltpu.SemaphoreType.DMA((heads,)),
        ],
        compiler_params=pltpu.CompilerParams(
            collective_id=0, has_side_effects=True, vmem_limit_bytes=63 << 20
        ),
        cost_estimate=pl.CostEstimate(flops=2 << 30, bytes_accessed=8 << 20, transcendentals=0),
    )(*args)


def solution(mesh):
    return jax.shard_map(
        functools.partial(shards, mesh.shape["seq"]),
        mesh=mesh,
        in_specs=(
            P(("groups", "seq"), "head"),
            P(("groups", "seq"), "head"),
            P(("groups", "seq"), "head"),
            P("head", None, ("groups", "seq")),
            P("head", None, ("groups", "seq")),
            P("head", "groups", None),
        ),
        out_specs=P(("groups", "seq"), "head"),
        check_vma=False,
    )
```

```python
import functools

import jax
import jax.numpy as jnp
from jax import lax
from jax.experimental import pallas as pl
from jax.experimental.pallas import tpu as pltpu
from jax.sharding import PartitionSpec as P

DH = 128
WEIGHTS = 16
F32 = jnp.float32
BF16 = jnp.bfloat16


def halves(x):
    high = x.astype(BF16)
    return high, (x - high.astype(F32)).astype(BF16)


def left(x, axis):
    high, low = halves(x)
    return jnp.concatenate([high, low, high], axis=axis)


def right(x, axis):
    high, low = halves(x)
    return jnp.concatenate([high, high, low], axis=axis)


def dot(a, b, dims):
    return lax.dot_general(a, b, (dims, ((), ())), preferred_element_type=F32)


def kernel(
    n, q_hbm, k_hbm, v_hbm, lw_hbm, pw_hbm, ps_hbm, o_hbm,
    q, k, v, lw, pw, ps, acc, wt, run, got, top,
    in_sem, send_sem, recv_sem, top_send, top_recv, out_sem,
):
    bits = n.bit_length() - 1
    stages = bits - 1
    rows = q.shape[0]
    heads = q.shape[1] // DH
    buckets = pw.shape[1]
    me = lax.axis_index("seq")

    def device(position):
        return {"seq": position}

    def cols(h):
        return pl.ds(pl.multiple_of(h * DH, DH), DH)

    def bit(b):
        return jnp.bitwise_and(jnp.right_shift(me, b), 1) == 1

    partners = [jnp.bitwise_xor(me, 1 << b) for b in range(stages)]
    source = (me >= n // 2 - 2) & (me < n // 2)
    upper = me >= n // 2
    onward = (me >= n // 2 - 2) & (me < n - 2)

    loads = [
        pltpu.make_async_copy(a, b, in_sem.at[i])
        for i, (a, b) in enumerate(
            [(k_hbm, k), (v_hbm, v), (q_hbm, q), (lw_hbm, lw), (pw_hbm, pw), (ps_hbm, ps)]
        )
    ]
    for load in loads:
        load.start()

    barrier = pltpu.get_barrier_semaphore()
    for partner in partners:
        pl.semaphore_signal(barrier, inc=1, device_id=device(partner))

    @pl.when(onward)
    def _():
        pl.semaphore_signal(barrier, inc=1, device_id=device(jnp.minimum(me + 2, n - 1)))

    @pl.when(upper)
    def _():
        pl.semaphore_signal(barrier, inc=1, device_id=device(jnp.maximum(me - 2, 0)))

    pl.semaphore_wait(barrier, stages + onward.astype(jnp.int32) + upper.astype(jnp.int32))

    def stage_copy(b, h):
        return pltpu.make_async_remote_copy(
            src_ref=run.at[b, h], dst_ref=got.at[b, h],
            send_sem=send_sem.at[b, h], recv_sem=recv_sem.at[b, h],
            device_id=device(partners[b]),
        )

    def sends(b):
        return jnp.logical_not(bit(b)) if 0 < b == stages - 1 else None

    def receives(b):
        return bit(b) if 0 < b == stages - 1 else None

    def when(cond, fn):
        if cond is None:
            fn()
        else:
            pl.when(cond)(fn)

    def onward_copy(src, h):
        return pltpu.make_async_remote_copy(
            src_ref=src, dst_ref=top.at[h],
            send_sem=top_send.at[0, h], recv_sem=top_recv.at[h],
            device_id=device(jnp.minimum(me + 2, n - 1)),
        )

    def cross_copy(h):
        return pltpu.make_async_remote_copy(
            src_ref=top.at[h], dst_ref=top.at[h],
            send_sem=top_send.at[1, h], recv_sem=top_recv.at[h],
            device_id=device(partners[0]),
        )

    mine = jnp.bitwise_and(me, 1)

    def owner(h):
        return jnp.bitwise_and(h, 1) == mine

    def ordered(j, first):
        early = j < heads // 2
        return jnp.where(early, 2 * j + first, 2 * j - heads + 1 - first)

    def arriving(j):
        return ordered(j, mine)

    def leaving(j):
        return ordered(j, 1 - mine)

    loads[0].wait()
    loads[1].wait()

    def states(j, _):
        h = leaving(j)
        kh = left(k[:, cols(h)], 0)
        vh = right(v[:, cols(h)], 0)
        run[0, h] = dot(kh, vh, ((0,), (0,)))
        stage_copy(0, h).start()
        return 0

    lax.fori_loop(0, heads, states, 0)

    for load in loads[2:]:
        load.wait()

    def add_level(h, state, index):
        qh = left(q[:, cols(h)], 1)
        acc[:, cols(h)] += wt[h, :, index : index + 1] * dot(qh, right(state, 0), ((1,), (0,)))

    def own(j):
        h = arriving(j)
        lv = jnp.concatenate(
            [pw[h]]
            + [lw[level, pl.ds(h, 1), :] for level in range(lw.shape[0])]
            + [jnp.zeros((WEIGHTS - buckets - lw.shape[0], rows), F32)],
            axis=0,
        )
        weights = lv.T
        wt[h, :, 0:WEIGHTS] = weights
        qh = left(q[:, cols(h)], 1)
        kh = right(k[:, cols(h)], 1)
        scores = dot(qh, kh, ((1,), (1,)))
        row = lax.broadcasted_iota(jnp.int32, (rows, rows), 0)
        col = lax.broadcasted_iota(jnp.int32, (rows, rows), 1)
        scores = jnp.where(col <= row, scores, 0.0)
        total = weights[:, buckets : buckets + 1] * dot(
            left(scores, 1), right(v[:, cols(h)], 0), ((1,), (0,))
        )
        for b in range(0, buckets, 2):
            pair = jnp.concatenate(
                [ps[h, c * DH : (c + 1) * DH, :] for c in (b, b + 1)], axis=1
            )
            both = dot(qh, right(pair, 0), ((1,), (0,)))
            total += weights[:, b : b + 1] * both[:, :DH]
            total += weights[:, b + 1 : b + 2] * both[:, DH:]
        acc[:, cols(h)] = total

    def stage(b, j):
        h = arriving(j)

        def arrived():
            stage_copy(b, h).wait_recv()
            if b < stages - 1:
                run[b + 1, h] = run[b, h] + got[b, h]
                when(sends(b + 1), lambda: stage_copy(b + 1, h).start())
            else:
                @pl.when(source & owner(h))
                def _():
                    run[b + 1, h] = run[b, h] + got[b, h]
                    onward_copy(run.at[b + 1, h], h).start()

        when(receives(b), arrived)

        @pl.when(bit(b))
        def _():
            add_level(h, got[b, h], buckets + 1 + b)

    def relay(j):
        h = jnp.minimum(2 * j + mine, heads - 1)

        @pl.when(upper & (j < heads // 2))
        def _():
            cross_copy(h).wait_recv()

            @pl.when(onward)
            def _():
                onward_copy(top.at[h], h).start()

            cross_copy(h).start()

    def out_copy(h):
        return pltpu.make_async_copy(acc.at[:, cols(h)], o_hbm.at[:, cols(h)], out_sem.at[h])

    def finish(j):
        h = arriving(j)

        @pl.when(upper)
        def _():
            @pl.when(jnp.logical_not(owner(h)))
            def _():
                cross_copy(h).wait_recv()

            add_level(h, top[h], buckets + stages + 1)

        out_copy(h).start()

    def at(h, fn):
        @pl.when((h >= 0) & (h < heads))
        def _():
            fn(h)

    def step(i, _):
        at(i, own)
        for b in range(stages):
            at(i - b, functools.partial(stage, b))
        at(i - stages, relay)
        at(i - stages - 2, finish)
        return 0

    lax.fori_loop(0, heads + stages + 2, step, 0)

    def drain(h, _):
        for b in range(stages):
            when(sends(b), lambda b=b: stage_copy(b, h).wait_send())

        @pl.when(onward & owner(h))
        def _():
            onward_copy(top.at[h], h).wait_send()

        @pl.when(upper & owner(h))
        def _():
            cross_copy(h).wait_send()

        out_copy(h).wait()
        return 0

    lax.fori_loop(0, heads, drain, 0)


def shards(n, queries, keys, values, level_weight, prefix_weight, prefix_state):
    rows, width = queries.shape
    heads = width // DH
    bits = n.bit_length() - 1
    stages = bits - 1
    by_level = jnp.transpose(level_weight, (1, 0, 2))
    args = (queries, keys, values, by_level, prefix_weight, prefix_state)
    state = (heads, DH, DH)
    return pl.pallas_call(
        functools.partial(kernel, n),
        out_shape=jax.ShapeDtypeStruct((rows, width), F32),
        in_specs=[pl.BlockSpec(memory_space=pl.ANY)] * len(args),
        out_specs=pl.BlockSpec(memory_space=pl.ANY),
        scratch_shapes=[pltpu.VMEM(a.shape, F32) for a in args]
        + [
            pltpu.VMEM((rows, width), F32),
            pltpu.VMEM((heads, rows, 128), F32),
            pltpu.VMEM((stages + 1,) + state, F32),
            pltpu.VMEM((stages,) + state, F32),
            pltpu.VMEM(state, F32),
            pltpu.SemaphoreType.DMA((len(args),)),
            pltpu.SemaphoreType.DMA((stages, heads)),
            pltpu.SemaphoreType.DMA((stages, heads)),
            pltpu.SemaphoreType.DMA((2, heads)),
            pltpu.SemaphoreType.DMA((heads,)),
            pltpu.SemaphoreType.DMA((heads,)),
        ],
        compiler_params=pltpu.CompilerParams(
            collective_id=0, has_side_effects=True, vmem_limit_bytes=63 << 20
        ),
        cost_estimate=pl.CostEstimate(flops=2 << 30, bytes_accessed=8 << 20, transcendentals=0),
    )(*args)


def solution(mesh):
    return jax.shard_map(
        functools.partial(shards, mesh.shape["seq"]),
        mesh=mesh,
        in_specs=(
            P(("groups", "seq"), "head"),
            P(("groups", "seq"), "head"),
            P(("groups", "seq"), "head"),
            P("head", None, ("groups", "seq")),
            P("head", None, ("groups", "seq")),
            P("head", "groups", None),
        ),
        out_specs=P(("groups", "seq"), "head"),
        check_vma=False,
    )
```

```python
import functools

import jax
import jax.numpy as jnp
from jax import lax
from jax.experimental import pallas as pl
from jax.experimental.pallas import tpu as pltpu
from jax.sharding import PartitionSpec as P

DH = 128
WEIGHTS = 16
F32 = jnp.float32
BF16 = jnp.bfloat16


def halves(x):
    high = x.astype(BF16)
    return high, (x - high.astype(F32)).astype(BF16)


def left(x, axis):
    high, low = halves(x)
    return jnp.concatenate([high, low, high], axis=axis)


def right(x, axis):
    high, low = halves(x)
    return jnp.concatenate([high, high, low], axis=axis)


def dot(a, b, dims):
    return lax.dot_general(a, b, (dims, ((), ())), preferred_element_type=F32)


def kernel(
    n, q_hbm, k_hbm, v_hbm, lw_hbm, pw_hbm, ps_hbm, acc,
    q, k, v, lw, pw, ps, wt, run, got, top,
    in_sem, send_sem, recv_sem, top_send, top_recv,
):
    bits = n.bit_length() - 1
    stages = bits - 1
    rows = q.shape[0]
    heads = q.shape[1] // DH
    buckets = pw.shape[1]
    me = lax.axis_index("seq")

    def device(position):
        return {"seq": position}

    def cols(h):
        return pl.ds(pl.multiple_of(h * DH, DH), DH)

    def bit(b):
        return jnp.bitwise_and(jnp.right_shift(me, b), 1) == 1

    partners = [jnp.bitwise_xor(me, 1 << b) for b in range(stages)]
    source = (me >= n // 2 - 2) & (me < n // 2)
    upper = me >= n // 2
    onward = (me >= n // 2 - 2) & (me < n - 2)

    loads = [
        pltpu.make_async_copy(a, b, in_sem.at[i])
        for i, (a, b) in enumerate(
            [(k_hbm, k), (v_hbm, v), (q_hbm, q), (lw_hbm, lw), (pw_hbm, pw), (ps_hbm, ps)]
        )
    ]
    for load in loads:
        load.start()

    barrier = pltpu.get_barrier_semaphore()
    for partner in partners:
        pl.semaphore_signal(barrier, inc=1, device_id=device(partner))

    @pl.when(onward)
    def _():
        pl.semaphore_signal(barrier, inc=1, device_id=device(jnp.minimum(me + 2, n - 1)))

    @pl.when(upper)
    def _():
        pl.semaphore_signal(barrier, inc=1, device_id=device(jnp.maximum(me - 2, 0)))

    pl.semaphore_wait(barrier, stages + onward.astype(jnp.int32) + upper.astype(jnp.int32))

    def stage_copy(b, h):
        return pltpu.make_async_remote_copy(
            src_ref=run.at[b, h], dst_ref=got.at[b, h],
            send_sem=send_sem.at[b, h], recv_sem=recv_sem.at[b, h],
            device_id=device(partners[b]),
        )

    last = me >= n - 2

    def sends(b):
        if b == 0 and stages <= 2:
            return jnp.logical_not(bit(0) & last)
        return jnp.logical_not(bit(b)) if 0 < b == stages - 1 else None

    def receives(b):
        if b == 0 and stages <= 2:
            return bit(0) | jnp.logical_not(last)
        return bit(b) if 0 < b == stages - 1 else None

    def when(cond, fn):
        if cond is None:
            fn()
        else:
            pl.when(cond)(fn)

    def onward_copy(src, h):
        return pltpu.make_async_remote_copy(
            src_ref=src, dst_ref=top.at[h],
            send_sem=top_send.at[0, h], recv_sem=top_recv.at[h],
            device_id=device(jnp.minimum(me + 2, n - 1)),
        )

    def cross_copy(h):
        return pltpu.make_async_remote_copy(
            src_ref=top.at[h], dst_ref=top.at[h],
            send_sem=top_send.at[1, h], recv_sem=top_recv.at[h],
            device_id=device(partners[0]),
        )

    mine = jnp.bitwise_and(me, 1)

    def owner(h):
        return jnp.bitwise_and(h, 1) == mine

    def ordered(j, first):
        early = j < heads // 2
        return jnp.where(early, 2 * j + first, 2 * j - heads + 1 - first)

    def arriving(j):
        return ordered(j, mine)

    def leaving(j):
        return ordered(j, 1 - mine)

    loads[0].wait()
    loads[1].wait()

    def states(j, _):
        h = leaving(j)
        kh = left(k[:, cols(h)], 0)
        vh = right(v[:, cols(h)], 0)
        run[0, h] = dot(kh, vh, ((0,), (0,)))
        when(sends(0), stage_copy(0, h).start)
        return 0

    lax.fori_loop(0, heads, states, 0)

    for load in loads[2:]:
        load.wait()

    def add_level(h, state, index):
        qh = left(q[:, cols(h)], 1)
        acc[:, cols(h)] += wt[h, :, index : index + 1] * dot(qh, right(state, 0), ((1,), (0,)))

    def own(j):
        h = arriving(j)
        lv = jnp.concatenate(
            [pw[h]]
            + [lw[level, pl.ds(h, 1), :] for level in range(lw.shape[0])]
            + [jnp.zeros((WEIGHTS - buckets - lw.shape[0], rows), F32)],
            axis=0,
        )
        weights = lv.T
        wt[h, :, 0:WEIGHTS] = weights
        qh = left(q[:, cols(h)], 1)
        kh = right(k[:, cols(h)], 1)
        scores = dot(qh, kh, ((1,), (1,)))
        row = lax.broadcasted_iota(jnp.int32, (rows, rows), 0)
        col = lax.broadcasted_iota(jnp.int32, (rows, rows), 1)
        scores = jnp.where(col <= row, scores, 0.0)
        total = weights[:, buckets : buckets + 1] * dot(
            left(scores, 1), right(v[:, cols(h)], 0), ((1,), (0,))
        )
        for b in range(0, buckets, 2):
            pair = jnp.concatenate(
                [ps[h, c * DH : (c + 1) * DH, :] for c in (b, b + 1)], axis=1
            )
            both = dot(qh, right(pair, 0), ((1,), (0,)))
            total += weights[:, b : b + 1] * both[:, :DH]
            total += weights[:, b + 1 : b + 2] * both[:, DH:]
        acc[:, cols(h)] = total

    def stage(b, j):
        h = arriving(j)

        def arrived():
            stage_copy(b, h).wait_recv()
            if b < stages - 1:
                run[b + 1, h] = run[b, h] + got[b, h]
                when(sends(b + 1), lambda: stage_copy(b + 1, h).start())
            else:
                @pl.when(source & owner(h))
                def _():
                    run[b + 1, h] = run[b, h] + got[b, h]
                    onward_copy(run.at[b + 1, h], h).start()

        when(receives(b), arrived)

        @pl.when(bit(b))
        def _():
            add_level(h, got[b, h], buckets + 1 + b)

    def relay(j):
        h = jnp.minimum(2 * j + mine, heads - 1)

        @pl.when(upper & (j < heads // 2))
        def _():
            cross_copy(h).wait_recv()

            @pl.when(onward)
            def _():
                onward_copy(top.at[h], h).start()

            cross_copy(h).start()

    def finish(j):
        h = arriving(j)

        @pl.when(upper)
        def _():
            @pl.when(jnp.logical_not(owner(h)))
            def _():
                cross_copy(h).wait_recv()

            add_level(h, top[h], buckets + stages + 1)

    def at(h, fn):
        @pl.when((h >= 0) & (h < heads))
        def _():
            fn(h)

    def step(i, _):
        at(i, own)
        for b in range(stages):
            at(i - b, functools.partial(stage, b))
        at(i - stages, relay)
        at(i - stages - 2, finish)
        return 0

    lax.fori_loop(0, heads + stages + 2, step, 0)

    def drain(h, _):
        for b in range(stages):
            when(sends(b), lambda b=b: stage_copy(b, h).wait_send())

        @pl.when(onward & owner(h))
        def _():
            onward_copy(top.at[h], h).wait_send()

        @pl.when(upper & owner(h))
        def _():
            cross_copy(h).wait_send()

        return 0

    lax.fori_loop(0, heads, drain, 0)


def shards(n, queries, keys, values, level_weight, prefix_weight, prefix_state):
    rows, width = queries.shape
    heads = width // DH
    bits = n.bit_length() - 1
    stages = bits - 1
    by_level = jnp.transpose(level_weight, (1, 0, 2))
    args = (queries, keys, values, by_level, prefix_weight, prefix_state)
    state = (heads, DH, DH)
    return pl.pallas_call(
        functools.partial(kernel, n),
        out_shape=pltpu.VMEM((rows, width), F32),
        in_specs=[pl.BlockSpec(memory_space=pl.ANY)] * len(args),
        out_specs=pl.BlockSpec(memory_space=pltpu.VMEM),
        scratch_shapes=[pltpu.VMEM(a.shape, F32) for a in args]
        + [
            pltpu.VMEM((heads, rows, 128), F32),
            pltpu.VMEM((stages + 1,) + state, F32),
            pltpu.VMEM((stages,) + state, F32),
            pltpu.VMEM(state, F32),
            pltpu.SemaphoreType.DMA((len(args),)),
            pltpu.SemaphoreType.DMA((stages, heads)),
            pltpu.SemaphoreType.DMA((stages, heads)),
            pltpu.SemaphoreType.DMA((2, heads)),
            pltpu.SemaphoreType.DMA((heads,)),
        ],
        compiler_params=pltpu.CompilerParams(
            collective_id=0, has_side_effects=True, vmem_limit_bytes=56 << 20
        ),
        cost_estimate=pl.CostEstimate(flops=2 << 30, bytes_accessed=8 << 20, transcendentals=0),
    )(*args)


def solution(mesh):
    return jax.shard_map(
        functools.partial(shards, mesh.shape["seq"]),
        mesh=mesh,
        in_specs=(
            P(("groups", "seq"), "head"),
            P(("groups", "seq"), "head"),
            P(("groups", "seq"), "head"),
            P("head", None, ("groups", "seq")),
            P("head", None, ("groups", "seq")),
            P("head", "groups", None),
        ),
        out_specs=P(("groups", "seq"), "head"),
        check_vma=False,
    )
```

```python
import functools

import jax
import jax.numpy as jnp
from jax import lax
from jax.experimental import pallas as pl
from jax.experimental.pallas import tpu as pltpu
from jax.sharding import PartitionSpec as P

DH = 128
WEIGHTS = 16
F32 = jnp.float32
BF16 = jnp.bfloat16


def halves(x):
    high = x.astype(BF16)
    return high, (x - high.astype(F32)).astype(BF16)


def left(x, axis):
    high, low = halves(x)
    return jnp.concatenate([high, low, high], axis=axis)


def right(x, axis):
    high, low = halves(x)
    return jnp.concatenate([high, high, low], axis=axis)


def dot(a, b, dims):
    return lax.dot_general(a, b, (dims, ((), ())), preferred_element_type=F32)


def kernel(
    n, q_hbm, k_hbm, v_hbm, lw_hbm, pw_hbm, ps_hbm, acc,
    q, k, v, lw, pw, ps, wt, run, got, top,
    in_sem, send_sem, recv_sem, top_send, top_recv,
):
    bits = n.bit_length() - 1
    stages = bits - 1
    rows = q.shape[0]
    heads = q.shape[1] // DH
    buckets = pw.shape[1]
    me = lax.axis_index("seq")

    def device(position):
        return {"seq": position}

    def cols(h):
        return pl.ds(pl.multiple_of(h * DH, DH), DH)

    def bit(b):
        return jnp.bitwise_and(jnp.right_shift(me, b), 1) == 1

    partners = [jnp.bitwise_xor(me, 1 << b) for b in range(stages)]
    source = (me >= n // 2 - 2) & (me < n // 2)
    upper = me >= n // 2
    onward = (me >= n // 2 - 2) & (me < n - 2)

    loads = [
        pltpu.make_async_copy(a, b, in_sem.at[i])
        for i, (a, b) in enumerate(
            [(k_hbm, k), (v_hbm, v), (q_hbm, q), (lw_hbm, lw), (pw_hbm, pw), (ps_hbm, ps)]
        )
    ]
    for load in loads:
        load.start()

    barrier = pltpu.get_barrier_semaphore()
    for partner in partners:
        pl.semaphore_signal(barrier, inc=1, device_id=device(partner))

    @pl.when(onward)
    def _():
        pl.semaphore_signal(barrier, inc=1, device_id=device(jnp.minimum(me + 2, n - 1)))

    @pl.when(upper)
    def _():
        pl.semaphore_signal(barrier, inc=1, device_id=device(jnp.maximum(me - 2, 0)))

    def stage_copy(b, h):
        return pltpu.make_async_remote_copy(
            src_ref=run.at[b, h], dst_ref=got.at[b, h],
            send_sem=send_sem.at[b, h], recv_sem=recv_sem.at[b, h],
            device_id=device(partners[b]),
        )

    last = me >= n - 2

    def sends(b):
        if b == 0 and stages <= 2:
            return jnp.logical_not(bit(0) & last)
        return jnp.logical_not(bit(b)) if 0 < b == stages - 1 else None

    def receives(b):
        if b == 0 and stages <= 2:
            return bit(0) | jnp.logical_not(last)
        return bit(b) if 0 < b == stages - 1 else None

    def when(cond, fn):
        if cond is None:
            fn()
        else:
            pl.when(cond)(fn)

    def onward_copy(src, h):
        return pltpu.make_async_remote_copy(
            src_ref=src, dst_ref=top.at[h],
            send_sem=top_send.at[0, h], recv_sem=top_recv.at[h],
            device_id=device(jnp.minimum(me + 2, n - 1)),
        )

    def cross_copy(h):
        return pltpu.make_async_remote_copy(
            src_ref=top.at[h], dst_ref=top.at[h],
            send_sem=top_send.at[1, h], recv_sem=top_recv.at[h],
            device_id=device(partners[0]),
        )

    mine = jnp.bitwise_and(me, 1)

    def owner(h):
        return jnp.bitwise_and(h, 1) == mine

    def ordered(j, first):
        early = j < heads // 2
        return jnp.where(early, 2 * j + first, 2 * j - heads + 1 - first)

    def arriving(j):
        return ordered(j, mine)

    def leaving(j):
        return ordered(j, 1 - mine)

    loads[0].wait()
    loads[1].wait()

    def own_state(h):
        kh = left(k[:, cols(h)], 0)
        vh = right(v[:, cols(h)], 0)
        run[0, h] = dot(kh, vh, ((0,), (0,)))

    own_state(leaving(0))
    pl.semaphore_wait(barrier, stages + onward.astype(jnp.int32) + upper.astype(jnp.int32))
    when(sends(0), lambda: stage_copy(0, leaving(0)).start())

    def states(j, _):
        h = leaving(j)
        own_state(h)
        when(sends(0), lambda: stage_copy(0, h).start())
        return 0

    lax.fori_loop(1, heads, states, 0)

    for load in loads[2:]:
        load.wait()

    def add_level(h, state, index):
        qh = left(q[:, cols(h)], 1)
        acc[:, cols(h)] += wt[h, :, index : index + 1] * dot(qh, right(state, 0), ((1,), (0,)))

    def own(j):
        h = arriving(j)
        lv = jnp.concatenate(
            [pw[h]]
            + [lw[level, pl.ds(h, 1), :] for level in range(lw.shape[0])]
            + [jnp.zeros((WEIGHTS - buckets - lw.shape[0], rows), F32)],
            axis=0,
        )
        weights = lv.T
        wt[h, :, 0:WEIGHTS] = weights
        qh = left(q[:, cols(h)], 1)
        kh = right(k[:, cols(h)], 1)
        scores = dot(qh, kh, ((1,), (1,)))
        row = lax.broadcasted_iota(jnp.int32, (rows, rows), 0)
        col = lax.broadcasted_iota(jnp.int32, (rows, rows), 1)
        scores = jnp.where(col <= row, scores, 0.0)
        total = weights[:, buckets : buckets + 1] * dot(
            left(scores, 1), right(v[:, cols(h)], 0), ((1,), (0,))
        )
        for b in range(0, buckets, 2):
            pair = jnp.concatenate(
                [ps[h, c * DH : (c + 1) * DH, :] for c in (b, b + 1)], axis=1
            )
            both = dot(qh, right(pair, 0), ((1,), (0,)))
            total += weights[:, b : b + 1] * both[:, :DH]
            total += weights[:, b + 1 : b + 2] * both[:, DH:]
        acc[:, cols(h)] = total

    def stage(b, j):
        h = arriving(j)

        def arrived():
            stage_copy(b, h).wait_recv()
            if b < stages - 1:
                run[b + 1, h] = run[b, h] + got[b, h]
                when(sends(b + 1), lambda: stage_copy(b + 1, h).start())
            else:
                @pl.when(source & owner(h))
                def _():
                    run[b + 1, h] = run[b, h] + got[b, h]
                    onward_copy(run.at[b + 1, h], h).start()

        when(receives(b), arrived)

    def level(b, j):
        h = arriving(j)

        @pl.when(bit(b))
        def _():
            add_level(h, got[b, h], buckets + 1 + b)

    def relay(j):
        h = jnp.minimum(2 * j + mine, heads - 1)

        @pl.when(upper & (j < heads // 2))
        def _():
            cross_copy(h).wait_recv()

            @pl.when(onward)
            def _():
                onward_copy(top.at[h], h).start()

            cross_copy(h).start()

    def finish(j):
        h = arriving(j)

        @pl.when(upper)
        def _():
            @pl.when(jnp.logical_not(owner(h)))
            def _():
                cross_copy(h).wait_recv()

            add_level(h, top[h], buckets + stages + 1)

    def at(h, fn):
        @pl.when((h >= 0) & (h < heads))
        def _():
            fn(h)

    own(0)

    def step(i, _):
        for b in range(stages):
            at(i - b, functools.partial(stage, b))
        at(i - stages, relay)
        at(i + 1, own)
        for b in range(stages):
            at(i - b, functools.partial(level, b))
        at(i - stages - 2, finish)
        return 0

    lax.fori_loop(0, heads + stages + 2, step, 0)

    def drain(h, _):
        for b in range(stages):
            when(sends(b), lambda b=b: stage_copy(b, h).wait_send())

        @pl.when(onward & owner(h))
        def _():
            onward_copy(top.at[h], h).wait_send()

        @pl.when(upper & owner(h))
        def _():
            cross_copy(h).wait_send()

        return 0

    lax.fori_loop(0, heads, drain, 0)


def shards(n, queries, keys, values, level_weight, prefix_weight, prefix_state):
    rows, width = queries.shape
    heads = width // DH
    bits = n.bit_length() - 1
    stages = bits - 1
    by_level = jnp.transpose(level_weight, (1, 0, 2))
    args = (queries, keys, values, by_level, prefix_weight, prefix_state)
    state = (heads, DH, DH)
    return pl.pallas_call(
        functools.partial(kernel, n),
        out_shape=pltpu.VMEM((rows, width), F32),
        in_specs=[pl.BlockSpec(memory_space=pl.ANY)] * len(args),
        out_specs=pl.BlockSpec(memory_space=pltpu.VMEM),
        scratch_shapes=[pltpu.VMEM(a.shape, F32) for a in args]
        + [
            pltpu.VMEM((heads, rows, 128), F32),
            pltpu.VMEM((stages + 1,) + state, F32),
            pltpu.VMEM((stages,) + state, F32),
            pltpu.VMEM(state, F32),
            pltpu.SemaphoreType.DMA((len(args),)),
            pltpu.SemaphoreType.DMA((stages, heads)),
            pltpu.SemaphoreType.DMA((stages, heads)),
            pltpu.SemaphoreType.DMA((2, heads)),
            pltpu.SemaphoreType.DMA((heads,)),
        ],
        compiler_params=pltpu.CompilerParams(
            collective_id=0, has_side_effects=True, vmem_limit_bytes=56 << 20
        ),
        cost_estimate=pl.CostEstimate(flops=2 << 30, bytes_accessed=8 << 20, transcendentals=0),
    )(*args)


def solution(mesh):
    return jax.shard_map(
        functools.partial(shards, mesh.shape["seq"]),
        mesh=mesh,
        in_specs=(
            P(("groups", "seq"), "head"),
            P(("groups", "seq"), "head"),
            P(("groups", "seq"), "head"),
            P("head", None, ("groups", "seq")),
            P("head", None, ("groups", "seq")),
            P("head", "groups", None),
        ),
        out_specs=P(("groups", "seq"), "head"),
        check_vma=False,
    )
```

```python
import functools

import jax
import jax.numpy as jnp
from jax import lax
from jax.experimental import pallas as pl
from jax.experimental.pallas import tpu as pltpu
from jax.sharding import PartitionSpec as P

DH = 128
WEIGHTS = 16
F32 = jnp.float32
BF16 = jnp.bfloat16


def halves(x):
    high = x.astype(BF16)
    return high, (x - high.astype(F32)).astype(BF16)


def left(x, axis):
    high, low = halves(x)
    return jnp.concatenate([high, low, high], axis=axis)


def right(x, axis):
    high, low = halves(x)
    return jnp.concatenate([high, high, low], axis=axis)


def dot(a, b, dims):
    return lax.dot_general(a, b, (dims, ((), ())), preferred_element_type=F32)


def kernel(
    n, q_hbm, k_hbm, v_hbm, lw_hbm, pw_hbm, ps_hbm, acc,
    q, k, v, lw, pw, ps, wt, run, got, top,
    in_sem, send_sem, recv_sem, top_send, top_recv,
):
    bits = n.bit_length() - 1
    stages = bits - 1
    rows = q.shape[0]
    heads = q.shape[1] // DH
    buckets = pw.shape[1]
    me = lax.axis_index("seq")

    def device(position):
        return {"seq": position}

    def cols(h):
        return pl.ds(pl.multiple_of(h * DH, DH), DH)

    def bit(b):
        return jnp.bitwise_and(jnp.right_shift(me, b), 1) == 1

    partners = [jnp.bitwise_xor(me, 1 << b) for b in range(stages)]
    source = (me >= n // 2 - 2) & (me < n // 2)
    upper = me >= n // 2
    onward = (me >= n // 2 - 2) & (me < n - 2)

    loads = [
        pltpu.make_async_copy(a, b, in_sem.at[i])
        for i, (a, b) in enumerate(
            [(k_hbm, k), (v_hbm, v), (q_hbm, q), (lw_hbm, lw), (pw_hbm, pw), (ps_hbm, ps)]
        )
    ]
    for load in loads:
        load.start()

    barrier = pltpu.get_barrier_semaphore()
    for partner in partners:
        pl.semaphore_signal(barrier, inc=1, device_id=device(partner))

    @pl.when(onward)
    def _():
        pl.semaphore_signal(barrier, inc=1, device_id=device(jnp.minimum(me + 2, n - 1)))

    @pl.when(upper)
    def _():
        pl.semaphore_signal(barrier, inc=1, device_id=device(jnp.maximum(me - 2, 0)))

    def stage_copy(b, h):
        return pltpu.make_async_remote_copy(
            src_ref=run.at[b, h], dst_ref=got.at[b, h],
            send_sem=send_sem.at[b, h], recv_sem=recv_sem.at[b, h],
            device_id=device(partners[b]),
        )

    last = me >= n - 2

    def sends(b):
        if b == 0 and stages <= 2:
            return jnp.logical_not(bit(0) & last)
        return jnp.logical_not(bit(b)) if 0 < b == stages - 1 else None

    def receives(b):
        if b == 0 and stages <= 2:
            return bit(0) | jnp.logical_not(last)
        return bit(b) if 0 < b == stages - 1 else None

    def when(cond, fn):
        if cond is None:
            fn()
        else:
            pl.when(cond)(fn)

    def onward_copy(src, h):
        return pltpu.make_async_remote_copy(
            src_ref=src, dst_ref=top.at[h],
            send_sem=top_send.at[0, h], recv_sem=top_recv.at[h],
            device_id=device(jnp.minimum(me + 2, n - 1)),
        )

    def cross_copy(h):
        return pltpu.make_async_remote_copy(
            src_ref=top.at[h], dst_ref=top.at[h],
            send_sem=top_send.at[1, h], recv_sem=top_recv.at[h],
            device_id=device(partners[0]),
        )

    mine = jnp.bitwise_and(me, 1)

    def owner(h):
        return jnp.bitwise_and(h, 1) == mine

    def ordered(j, first):
        early = j < heads // 2
        return jnp.where(early, 2 * j + first, 2 * j - heads + 1 - first)

    def arriving(j):
        return ordered(j, mine)

    def leaving(j):
        return ordered(j, 1 - mine)

    loads[0].wait()
    loads[1].wait()

    def own_state(h):
        kh = left(k[:, cols(h)], 0)
        vh = right(v[:, cols(h)], 0)
        run[0, h] = dot(kh, vh, ((0,), (0,)))

    own_state(leaving(0))
    pl.semaphore_wait(barrier, stages + onward.astype(jnp.int32) + upper.astype(jnp.int32))
    when(sends(0), lambda: stage_copy(0, leaving(0)).start())

    def states(j, _):
        h = leaving(j)
        own_state(h)
        when(sends(0), lambda: stage_copy(0, h).start())
        return 0

    lax.fori_loop(1, heads, states, 0)

    for load in loads[2:]:
        load.wait()

    def add_level(h, state, index):
        qh = left(q[:, cols(h)], 1)
        acc[:, cols(h)] += wt[h, :, index : index + 1] * dot(qh, right(state, 0), ((1,), (0,)))

    def own(j):
        h = arriving(j)
        lv = jnp.concatenate(
            [pw[h]]
            + [lw[level, pl.ds(h, 1), :] for level in range(lw.shape[0])]
            + [jnp.zeros((WEIGHTS - buckets - lw.shape[0], rows), F32)],
            axis=0,
        )
        weights = lv.T
        wt[h, :, 0:WEIGHTS] = weights
        qh = left(q[:, cols(h)], 1)
        kh = right(k[:, cols(h)], 1)
        scores = dot(qh, kh, ((1,), (1,)))
        row = lax.broadcasted_iota(jnp.int32, (rows, rows), 0)
        col = lax.broadcasted_iota(jnp.int32, (rows, rows), 1)
        scores = jnp.where(col <= row, scores, 0.0)
        total = weights[:, buckets : buckets + 1] * dot(
            left(scores, 1), right(v[:, cols(h)], 0), ((1,), (0,))
        )
        for b in range(0, buckets, 2):
            pair = jnp.concatenate(
                [ps[h, c * DH : (c + 1) * DH, :] for c in (b, b + 1)], axis=1
            )
            both = dot(qh, right(pair, 0), ((1,), (0,)))
            total += weights[:, b : b + 1] * both[:, :DH]
            total += weights[:, b + 1 : b + 2] * both[:, DH:]
        acc[:, cols(h)] = total

    def stage(b, j):
        h = arriving(j)

        def arrived():
            stage_copy(b, h).wait_recv()
            if b < stages - 1:
                run[b + 1, h] = run[b, h] + got[b, h]
                when(sends(b + 1), lambda: stage_copy(b + 1, h).start())
            else:
                @pl.when(source & owner(h))
                def _():
                    run[b + 1, h] = run[b, h] + got[b, h]
                    onward_copy(run.at[b + 1, h], h).start()

        when(receives(b), arrived)

    def level(b, j):
        h = arriving(j)

        @pl.when(bit(b))
        def _():
            add_level(h, got[b, h], buckets + 1 + b)

    def relay(j):
        h = jnp.minimum(2 * j + mine, heads - 1)

        @pl.when(upper & (j < heads // 2))
        def _():
            cross_copy(h).wait_recv()

            @pl.when(onward)
            def _():
                onward_copy(top.at[h], h).start()

            cross_copy(h).start()

    def finish(j):
        h = arriving(j)

        @pl.when(upper)
        def _():
            @pl.when(jnp.logical_not(owner(h)))
            def _():
                cross_copy(h).wait_recv()

            add_level(h, top[h], buckets + stages + 1)

    def at(h, fn):
        @pl.when((h >= 0) & (h < heads))
        def _():
            fn(h)

    def step(i, _):
        at(i, own)
        for b in range(stages):
            at(i - b, functools.partial(stage, b))
        at(i - stages, relay)
        for b in range(stages):
            at(i - b, functools.partial(level, b))
        at(i - stages - 2, finish)
        return 0

    lax.fori_loop(0, heads + stages + 2, step, 0)

    def drain(h, _):
        for b in range(stages):
            when(sends(b), lambda b=b: stage_copy(b, h).wait_send())

        @pl.when(onward & owner(h))
        def _():
            onward_copy(top.at[h], h).wait_send()

        @pl.when(upper & owner(h))
        def _():
            cross_copy(h).wait_send()

        return 0

    lax.fori_loop(0, heads, drain, 0)


def shards(n, queries, keys, values, level_weight, prefix_weight, prefix_state):
    rows, width = queries.shape
    heads = width // DH
    bits = n.bit_length() - 1
    stages = bits - 1
    by_level = jnp.transpose(level_weight, (1, 0, 2))
    args = (queries, keys, values, by_level, prefix_weight, prefix_state)
    state = (heads, DH, DH)
    return pl.pallas_call(
        functools.partial(kernel, n),
        out_shape=pltpu.VMEM((rows, width), F32),
        in_specs=[pl.BlockSpec(memory_space=pl.ANY)] * len(args),
        out_specs=pl.BlockSpec(memory_space=pltpu.VMEM),
        scratch_shapes=[pltpu.VMEM(a.shape, F32) for a in args]
        + [
            pltpu.VMEM((heads, rows, 128), F32),
            pltpu.VMEM((stages + 1,) + state, F32),
            pltpu.VMEM((stages,) + state, F32),
            pltpu.VMEM(state, F32),
            pltpu.SemaphoreType.DMA((len(args),)),
            pltpu.SemaphoreType.DMA((stages, heads)),
            pltpu.SemaphoreType.DMA((stages, heads)),
            pltpu.SemaphoreType.DMA((2, heads)),
            pltpu.SemaphoreType.DMA((heads,)),
        ],
        compiler_params=pltpu.CompilerParams(
            collective_id=0, has_side_effects=True, vmem_limit_bytes=56 << 20
        ),
        cost_estimate=pl.CostEstimate(flops=2 << 30, bytes_accessed=8 << 20, transcendentals=0),
    )(*args)


def solution(mesh):
    return jax.shard_map(
        functools.partial(shards, mesh.shape["seq"]),
        mesh=mesh,
        in_specs=(
            P(("groups", "seq"), "head"),
            P(("groups", "seq"), "head"),
            P(("groups", "seq"), "head"),
            P("head", None, ("groups", "seq")),
            P("head", None, ("groups", "seq")),
            P("head", "groups", None),
        ),
        out_specs=P(("groups", "seq"), "head"),
        check_vma=False,
    )
```

```python
import functools

import jax
import jax.numpy as jnp
from jax import lax
from jax.experimental import pallas as pl
from jax.experimental.pallas import tpu as pltpu
from jax.sharding import PartitionSpec as P

DH = 128
WEIGHTS = 16
F32 = jnp.float32
BF16 = jnp.bfloat16


def halves(x):
    high = x.astype(BF16)
    return high, (x - high.astype(F32)).astype(BF16)


def left(x, axis):
    high, low = halves(x)
    return jnp.concatenate([high, low, high], axis=axis)


def right(x, axis):
    high, low = halves(x)
    return jnp.concatenate([high, high, low], axis=axis)


def dot(a, b, dims):
    return lax.dot_general(a, b, (dims, ((), ())), preferred_element_type=F32)


def kernel(
    n, q_hbm, k_hbm, v_hbm, lw_hbm, pw_hbm, ps_hbm, acc,
    q, k, v, lw, pw, ps, wt, run, got, top,
    in_sem, send_sem, recv_sem, top_send, top_recv,
):
    bits = n.bit_length() - 1
    stages = bits - 1
    rows = q.shape[0]
    heads = q.shape[1] // DH
    buckets = pw.shape[1]
    me = lax.axis_index("seq")

    def device(position):
        return {"seq": position}

    def cols(h):
        return pl.ds(pl.multiple_of(h * DH, DH), DH)

    def bit(b):
        return jnp.bitwise_and(jnp.right_shift(me, b), 1) == 1

    partners = [jnp.bitwise_xor(me, 1 << b) for b in range(stages)]
    source = (me >= n // 2 - 2) & (me < n // 2)
    upper = me >= n // 2
    onward = (me >= n // 2 - 2) & (me < n - 2)

    loads = [
        pltpu.make_async_copy(a, b, in_sem.at[i])
        for i, (a, b) in enumerate(
            [(k_hbm, k), (v_hbm, v), (q_hbm, q), (lw_hbm, lw), (pw_hbm, pw), (ps_hbm, ps)]
        )
    ]
    for load in loads[:2]:
        load.start()

    barrier = pltpu.get_barrier_semaphore()
    for partner in partners:
        pl.semaphore_signal(barrier, inc=1, device_id=device(partner))

    @pl.when(onward)
    def _():
        pl.semaphore_signal(barrier, inc=1, device_id=device(jnp.minimum(me + 2, n - 1)))

    @pl.when(upper)
    def _():
        pl.semaphore_signal(barrier, inc=1, device_id=device(jnp.maximum(me - 2, 0)))

    def stage_copy(b, h):
        return pltpu.make_async_remote_copy(
            src_ref=run.at[b, h], dst_ref=got.at[b, h],
            send_sem=send_sem.at[b, h], recv_sem=recv_sem.at[b, h],
            device_id=device(partners[b]),
        )

    last = me >= n - 2

    def sends(b):
        if b == 0 and stages <= 2:
            return jnp.logical_not(bit(0) & last)
        return jnp.logical_not(bit(b)) if 0 < b == stages - 1 else None

    def receives(b):
        if b == 0 and stages <= 2:
            return bit(0) | jnp.logical_not(last)
        return bit(b) if 0 < b == stages - 1 else None

    def when(cond, fn):
        if cond is None:
            fn()
        else:
            pl.when(cond)(fn)

    def onward_copy(src, h):
        return pltpu.make_async_remote_copy(
            src_ref=src, dst_ref=top.at[h],
            send_sem=top_send.at[0, h], recv_sem=top_recv.at[h],
            device_id=device(jnp.minimum(me + 2, n - 1)),
        )

    def cross_copy(h):
        return pltpu.make_async_remote_copy(
            src_ref=top.at[h], dst_ref=top.at[h],
            send_sem=top_send.at[1, h], recv_sem=top_recv.at[h],
            device_id=device(partners[0]),
        )

    mine = jnp.bitwise_and(me, 1)

    def owner(h):
        return jnp.bitwise_and(h, 1) == mine

    def ordered(j, first):
        early = j < heads // 2
        return jnp.where(early, 2 * j + first, 2 * j - heads + 1 - first)

    def arriving(j):
        return ordered(j, mine)

    def leaving(j):
        return ordered(j, 1 - mine)

    loads[0].wait()
    loads[1].wait()
    for load in loads[2:]:
        load.start()

    def own_state(h):
        kh = left(k[:, cols(h)], 0)
        vh = right(v[:, cols(h)], 0)
        run[0, h] = dot(kh, vh, ((0,), (0,)))

    own_state(leaving(0))
    pl.semaphore_wait(barrier, stages + onward.astype(jnp.int32) + upper.astype(jnp.int32))
    when(sends(0), lambda: stage_copy(0, leaving(0)).start())

    def states(j, _):
        h = leaving(j)
        own_state(h)
        when(sends(0), lambda: stage_copy(0, h).start())
        return 0

    lax.fori_loop(1, heads, states, 0)

    for load in loads[2:]:
        load.wait()

    def add_level(h, state, index):
        qh = left(q[:, cols(h)], 1)
        acc[:, cols(h)] += wt[h, :, index : index + 1] * dot(qh, right(state, 0), ((1,), (0,)))

    def own(j):
        h = arriving(j)
        lv = jnp.concatenate(
            [pw[h]]
            + [lw[level, pl.ds(h, 1), :] for level in range(lw.shape[0])]
            + [jnp.zeros((WEIGHTS - buckets - lw.shape[0], rows), F32)],
            axis=0,
        )
        weights = lv.T
        wt[h, :, 0:WEIGHTS] = weights
        qh = left(q[:, cols(h)], 1)
        kh = right(k[:, cols(h)], 1)
        scores = dot(qh, kh, ((1,), (1,)))
        row = lax.broadcasted_iota(jnp.int32, (rows, rows), 0)
        col = lax.broadcasted_iota(jnp.int32, (rows, rows), 1)
        scores = jnp.where(col <= row, scores, 0.0)
        total = weights[:, buckets : buckets + 1] * dot(
            left(scores, 1), right(v[:, cols(h)], 0), ((1,), (0,))
        )
        for b in range(0, buckets, 2):
            pair = jnp.concatenate(
                [ps[h, c * DH : (c + 1) * DH, :] for c in (b, b + 1)], axis=1
            )
            both = dot(qh, right(pair, 0), ((1,), (0,)))
            total += weights[:, b : b + 1] * both[:, :DH]
            total += weights[:, b + 1 : b + 2] * both[:, DH:]
        acc[:, cols(h)] = total

    def stage(b, j):
        h = arriving(j)

        def arrived():
            stage_copy(b, h).wait_recv()
            if b < stages - 1:
                run[b + 1, h] = run[b, h] + got[b, h]
                when(sends(b + 1), lambda: stage_copy(b + 1, h).start())
            else:
                @pl.when(source & owner(h))
                def _():
                    run[b + 1, h] = run[b, h] + got[b, h]
                    onward_copy(run.at[b + 1, h], h).start()

        when(receives(b), arrived)

    def level(b, j):
        h = arriving(j)

        @pl.when(bit(b))
        def _():
            add_level(h, got[b, h], buckets + 1 + b)

    def relay(j):
        h = jnp.minimum(2 * j + mine, heads - 1)

        @pl.when(upper & (j < heads // 2))
        def _():
            cross_copy(h).wait_recv()

            @pl.when(onward)
            def _():
                onward_copy(top.at[h], h).start()

            cross_copy(h).start()

    def finish(j):
        h = arriving(j)

        @pl.when(upper)
        def _():
            @pl.when(jnp.logical_not(owner(h)))
            def _():
                cross_copy(h).wait_recv()

            add_level(h, top[h], buckets + stages + 1)

    def at(h, fn):
        @pl.when((h >= 0) & (h < heads))
        def _():
            fn(h)

    def step(i, _):
        at(i, own)
        for b in range(stages):
            at(i - b, functools.partial(stage, b))
            at(i - b, functools.partial(level, b))
        at(i - stages, relay)
        at(i - stages - 2, finish)
        return 0

    lax.fori_loop(0, heads + stages + 2, step, 0)

    def drain(h, _):
        for b in range(stages):
            when(sends(b), lambda b=b: stage_copy(b, h).wait_send())

        @pl.when(onward & owner(h))
        def _():
            onward_copy(top.at[h], h).wait_send()

        @pl.when(upper & owner(h))
        def _():
            cross_copy(h).wait_send()

        return 0

    lax.fori_loop(0, heads, drain, 0)


def shards(n, queries, keys, values, level_weight, prefix_weight, prefix_state):
    rows, width = queries.shape
    heads = width // DH
    bits = n.bit_length() - 1
    stages = bits - 1
    by_level = jnp.transpose(level_weight, (1, 0, 2))
    args = (queries, keys, values, by_level, prefix_weight, prefix_state)
    state = (heads, DH, DH)
    return pl.pallas_call(
        functools.partial(kernel, n),
        out_shape=pltpu.VMEM((rows, width), F32),
        in_specs=[pl.BlockSpec(memory_space=pl.ANY)] * len(args),
        out_specs=pl.BlockSpec(memory_space=pltpu.VMEM),
        scratch_shapes=[pltpu.VMEM(a.shape, F32) for a in args]
        + [
            pltpu.VMEM((heads, rows, 128), F32),
            pltpu.VMEM((stages + 1,) + state, F32),
            pltpu.VMEM((stages,) + state, F32),
            pltpu.VMEM(state, F32),
            pltpu.SemaphoreType.DMA((len(args),)),
            pltpu.SemaphoreType.DMA((stages, heads)),
            pltpu.SemaphoreType.DMA((stages, heads)),
            pltpu.SemaphoreType.DMA((2, heads)),
            pltpu.SemaphoreType.DMA((heads,)),
        ],
        compiler_params=pltpu.CompilerParams(
            collective_id=0, has_side_effects=True, vmem_limit_bytes=56 << 20
        ),
        cost_estimate=pl.CostEstimate(flops=2 << 30, bytes_accessed=8 << 20, transcendentals=0),
    )(*args)


def solution(mesh):
    return jax.shard_map(
        functools.partial(shards, mesh.shape["seq"]),
        mesh=mesh,
        in_specs=(
            P(("groups", "seq"), "head"),
            P(("groups", "seq"), "head"),
            P(("groups", "seq"), "head"),
            P("head", None, ("groups", "seq")),
            P("head", None, ("groups", "seq")),
            P("head", "groups", None),
        ),
        out_specs=P(("groups", "seq"), "head"),
        check_vma=False,
    )
```
